32 devices in a mesh: dp: 8 (over y, x, core), tensor: 4 (over z).
Axes of the slice: x: 2, y: 2, z: 4, core: 2. Of those that a mesh axis runs over, the one named last changes fastest.
Arguments:
- gate_pre: bfloat16 [4096, 3584], P('dp', 'tensor'), may hold values from -6 to 6
- up_pre: bfloat16 [4096, 3584], P('dp', 'tensor'), may hold values from -6 to 6
- down_weight: bfloat16 [3584, 4096], P('tensor'), may hold values from -0.09375 to 0.09375
- grad_out: bfloat16 [4096, 4096], P(('dp', 'tensor')), may hold values from -6 to 6
Outputs:
- ffn_out: bfloat16 [4096, 4096], P(('dp', 'tensor'))
- grad_gate: bfloat16 [4096, 3584], P('dp', 'tensor')
- grad_up: bfloat16 [4096, 3584], P('dp', 'tensor')
- grad_down: float32 [3584, 4096], P('tensor', 'dp')
The draws below stay inside these ranges and needn't reach their ends.
All inputs are finite; a program needn't handle non-finite values.
Results may differ from the reference program's by a relative error of at most 0.017.
Values may be sent and summed in bfloat16 or wider, within the bound.
No kernel may reach another device: no remote copies, remote signals or barrier semaphores. Data moves between devices by JAX's collectives and lax.ppermute only.
A program may use at most 128 MiB of HBM per device.

```python
import math
import jax
import jax.numpy as jnp
from jax import lax

D = 4096
FF_DEV = 896
TOK_DEV = 128
FF = 3584
TOKENS = 4096
N_DP = 8
N_TENSOR = 4


def with_spikes(array, own_key, source, target, shards_of, factor):
    def block_of(dim):
        return (jnp.arange(array.shape[dim]) // (array.shape[dim] // shards_of)).reshape((-1,) + (1,) * (array.ndim - 1 - dim))

    one_side = jax.random.permutation(own_key, shards_of)[block_of(target)]
    far = (block_of(target) + shards_of // 2) % shards_of
    return jnp.where((block_of(source) == one_side) | (block_of(source) == far), factor * array, array)


def shard_levels(key, shape, split, least, high):
    factor_of, own = 1.0, jax.random.fold_in(key, 6)
    for position, blocks in split:
        heights = jnp.exp(jax.random.uniform(jax.random.fold_in(own, position), (blocks,), jnp.float32, least / len(split), high / len(split)))
        factor_of = factor_of * jnp.repeat(heights, shape[position] // blocks).reshape([-1 if axis == position else 1 for axis in range(len(shape))])
    return factor_of


def gaussian(stream_key, dims, scale, bound, split=(), dtype=jnp.bfloat16):
    drawn = scale * jax.random.normal(stream_key, dims, jnp.float32)
    if split:
        drawn = drawn * shard_levels(stream_key, dims, split, -0.22, 0.18)
    return jnp.clip(drawn, -bound, bound).astype(dtype)


def heavy_noise(own_key, shape, width, bound, cuts, heavy, dtype=jnp.bfloat16):
    result = width * jax.random.normal(own_key, shape, jnp.float32)
    if cuts:
        result = result * shard_levels(own_key, shape, cuts, -0.22, 0.18)
    return jnp.clip(with_spikes(result, jax.random.fold_in(own_key, 3), *heavy), -bound, bound).astype(dtype)


def setup_inputs(seed: int = 0) -> dict:
    key_of = jax.random.split(jax.random.key(seed), 5)
    gate_pre = gaussian(key_of[0], (TOKENS, FF), 1.0, 6.0, ((0, 8), (1, 4)))
    up_pre = gaussian(key_of[1], (TOKENS, FF), 1.0, 6.0, ((0, 8), (1, 4)))
    down_weight = gaussian(key_of[2], (FF, D), FF ** -0.5, 0.09375, ((0, 4),))
    grad_out = heavy_noise(key_of[3], (TOKENS, D), 1.0, 6.0, ((0, 32),), (0, 1, 32, 2.75))
    return dict(gate_pre=gate_pre, up_pre=up_pre, down_weight=down_weight, grad_out=grad_out)


def reference(gate_pre, up_pre, down_weight, grad_out):
    gate_val = gate_pre.astype(jnp.float32)
    up_val = up_pre.astype(jnp.float32)
    sigmoid_gate = jax.nn.sigmoid(gate_val)
    activated = gate_val * sigmoid_gate
    hidden = (activated * up_val).astype(jnp.bfloat16)
    hidden_blocks = hidden.reshape(TOKENS, N_TENSOR, FF_DEV).transpose(1, 0, 2)
    weight_blocks = down_weight.reshape(N_TENSOR, FF_DEV, D)

    def add_partial(total, pair):
        block_rows, block_weight = pair
        partial_value = jnp.dot(block_rows, block_weight, preferred_element_type=jnp.float32)
        return (total + partial_value.astype(jnp.bfloat16).astype(jnp.float32), None)
    output_sum, _ = lax.scan(add_partial, jnp.zeros((TOKENS, D), jnp.float32), (hidden_blocks, weight_blocks))
    ffn_out = output_sum.astype(jnp.bfloat16)
    hidden_grad = jnp.dot(grad_out, down_weight.T, preferred_element_type=jnp.float32)
    grad_gate = (hidden_grad * up_val * sigmoid_gate * (1.0 + gate_val * (1.0 - sigmoid_gate))).astype(jnp.bfloat16)
    grad_up = (hidden_grad * activated).astype(jnp.bfloat16)
    grad_scale = 1.0 / math.sqrt(TOKENS)
    replica_rows = TOK_DEV * N_TENSOR
    hidden_reps = hidden.reshape(N_DP, replica_rows, FF)
    cotangent_reps = grad_out.reshape(N_DP, replica_rows, D)

    def add_replica(total, pair):
        rep_hidden, rep_cotangent = pair
        product = jnp.dot(rep_hidden.T, rep_cotangent, preferred_element_type=jnp.float32) * grad_scale
        return (total + product.astype(jnp.bfloat16).astype(jnp.float32), None)
    grad_down, _ = lax.scan(add_replica, jnp.zeros((FF, D), jnp.float32), (hidden_reps, cotangent_reps))
    return (ffn_out, grad_gate, grad_up, grad_down)
```

```python
import functools
import math

import jax
import jax.numpy as jnp
from jax import lax
from jax.experimental import pallas as pl
from jax.experimental.pallas import tpu as pltpu
from jax.sharding import PartitionSpec as P

F32, BF16 = jnp.float32, jnp.bfloat16
VMEM_BYTES = 48 * 1024 * 1024


def plain_body(gate_pre, up_pre, down_weight, grad_out):
    gate_val = gate_pre.astype(F32)
    up_val = up_pre.astype(F32)
    sigmoid_gate = jax.nn.sigmoid(gate_val)
    activated = gate_val * sigmoid_gate
    hidden = (activated * up_val).astype(BF16)
    grad_scale = 1.0 / math.sqrt(hidden.shape[0] * lax.axis_size("dp"))
    ffn_out = lax.psum_scatter(
        jnp.dot(hidden, down_weight, preferred_element_type=F32).astype(BF16),
        "tensor",
        scatter_dimension=0,
        tiled=True,
    )
    piece = lax.all_gather(grad_out, "tensor", axis=0, tiled=True)
    hidden_grad = jnp.einsum("td,fd->tf", piece, down_weight, preferred_element_type=F32)
    weight_grad = jnp.einsum("tf,td->fd", hidden, piece, preferred_element_type=F32)
    grad_down = lax.psum_scatter(
        (weight_grad * grad_scale).astype(BF16), "dp", scatter_dimension=1, tiled=True
    ).astype(F32)
    grad_gate = (
        hidden_grad * up_val * sigmoid_gate * (1.0 + gate_val * (1.0 - sigmoid_gate))
    ).astype(BF16)
    grad_up = (hidden_grad * activated).astype(BF16)
    return (ffn_out, grad_gate, grad_up, grad_down)


OUTER = [(0, 1), (1, 0), (2, 3), (3, 2)]
OUTWARD = [(1, 0), (2, 3)]
INWARD = [(0, 1), (3, 2)]
MIDDLE = [(1, 2), (2, 1)]


def hidden_kernel(place, gate_ref, up_ref, hidden_ref, turned_ref):
    gate_val = gate_ref[...].astype(F32)
    hidden = gate_val * jax.nn.sigmoid(gate_val) * up_ref[...].astype(F32)
    hidden_ref[...] = hidden.astype(BF16)
    turned_ref[...] = hidden.T.astype(BF16)


def hidden_of(place, gate_pre, up_pre):
    rows, width = gate_pre.shape
    block = rows // 4
    return pl.pallas_call(
        hidden_kernel,
        grid_spec=pltpu.PrefetchScalarGridSpec(
            num_scalar_prefetch=1,
            grid=(4,),
            in_specs=[pl.BlockSpec((block, width), lambda i, place: (place[i], 0))] * 2,
            out_specs=[
                pl.BlockSpec((block, width), lambda i, place: (i, 0)),
                pl.BlockSpec((width, block), lambda i, place: (0, i)),
            ],
        ),
        out_shape=[
            jax.ShapeDtypeStruct((rows, width), BF16),
            jax.ShapeDtypeStruct((width, rows), BF16),
        ],
        cost_estimate=pl.CostEstimate(flops=10 * rows * width, bytes_accessed=8 * rows * width, transcendentals=rows * width),
        compiler_params=pltpu.CompilerParams(vmem_limit_bytes=VMEM_BYTES),
        name="hidden",
    )(place, gate_pre, up_pre)


def forward_kernel(hidden_ref, weight_ref, *out_refs):
    block = out_refs[0].shape[0]
    product = jnp.dot(hidden_ref[...], weight_ref[...], preferred_element_type=F32)
    for i, out_ref in enumerate(out_refs):
        out_ref[...] = product[i * block : (i + 1) * block].astype(BF16)


def forward_of(hidden, weight, tile=512):
    rows, width = hidden.shape
    model = weight.shape[1]
    block = rows // 4
    return pl.pallas_call(
        forward_kernel,
        grid=(model // tile,),
        in_specs=[
            pl.BlockSpec((rows, width), lambda j: (0, 0)),
            pl.BlockSpec((width, tile), lambda j: (0, j)),
        ],
        out_specs=[pl.BlockSpec((block, tile), lambda j: (0, j))] * 4,
        out_shape=[jax.ShapeDtypeStruct((block, model), BF16)] * 4,
        cost_estimate=pl.CostEstimate(
            flops=2 * rows * width * model, bytes_accessed=2 * (rows * model + width * model), transcendentals=0
        ),
        compiler_params=pltpu.CompilerParams(vmem_limit_bytes=VMEM_BYTES),
        name="forward",
    )(hidden, weight)


def gathered(edge, own, outer, mid_e, mid_m, far_e, far_m):
    return jnp.concatenate(
        [
            own[...],
            outer[...],
            jnp.where(edge, mid_e[...], mid_m[...]),
            jnp.where(edge, far_e[...], far_m[...]),
        ],
        axis=0,
    )


def weight_kernel(scale, place, turned_ref, *refs):
    out_ref = refs[6]
    piece = gathered(place[4] == 1, *refs[:6])
    product = jnp.dot(turned_ref[...], piece, preferred_element_type=F32)
    out_ref[0] = (product * scale).astype(BF16)


def weight_grad_of(place, turned, blocks, scale, odd, n_dp):
    width, rows = turned.shape
    block, columns = blocks[0].shape
    tile = columns // n_dp
    return pl.pallas_call(
        functools.partial(weight_kernel, scale),
        grid_spec=pltpu.PrefetchScalarGridSpec(
            num_scalar_prefetch=1,
            grid=(n_dp // 2,),
            in_specs=[pl.BlockSpec((width, rows), lambda i, place: (0, 0))]
            + [pl.BlockSpec((block, tile), lambda i, place: (0, jnp.bitwise_xor(place[5], 2 * i + odd)))] * 6,
            out_specs=pl.BlockSpec((1, width, tile), lambda i, place: (i, 0, 0)),
        ),
        out_shape=jax.ShapeDtypeStruct((n_dp // 2, width, tile), BF16),
        cost_estimate=pl.CostEstimate(
            flops=rows * width * columns, bytes_accessed=width * columns + 3 * rows * columns // 2, transcendentals=0
        ),
        compiler_params=pltpu.CompilerParams(vmem_limit_bytes=VMEM_BYTES),
        name="weight_grad",
    )(place, turned, *blocks)


def input_kernel(tiles, place, weight_ref, gate_ref, up_ref, *refs):
    step = pl.program_id(0)
    grad_gate_ref, grad_up_ref, total_ref = refs[-3:]
    edge = place[4] == 1
    start, part = 0, None
    for n, tile in enumerate(tiles):
        piece = gathered(edge, *refs[6 * n : 6 * n + 6])
        product = lax.dot_general(
            piece, weight_ref[:, start : start + tile], (((1,), (1,)), ((), ())), preferred_element_type=F32
        )
        part = product if part is None else part + product
        start += tile

    @pl.when(step == 0)
    def _():
        total_ref[...] = part

    @pl.when(step > 0)
    def _():
        total_ref[...] += part

    @pl.when(step == pl.num_programs(0) - 1)
    def _():
        block = total_ref.shape[0] // 4
        for i in range(4):
            rows = pl.ds(pl.multiple_of(place[i] * block, block), block)
            hidden_grad = total_ref[i * block : (i + 1) * block]
            gate_val = gate_ref[rows].astype(F32)
            up_val = up_ref[rows].astype(F32)
            s = jax.nn.sigmoid(gate_val)
            grad_gate_ref[rows] = (hidden_grad * up_val * s * (1.0 + gate_val * (1.0 - s))).astype(BF16)
            grad_up_ref[rows] = (hidden_grad * (gate_val * s)).astype(BF16)


def input_grads_of(place, weight, gate_pre, up_pre, parts, n_dp):
    rows, width = gate_pre.shape
    model = weight.shape[1]
    tiles = [blocks[0].shape[1] // n_dp for blocks in parts]
    whole = pl.BlockSpec((rows, width), lambda j, place: (0, 0))
    return pl.pallas_call(
        functools.partial(input_kernel, tiles),
        grid_spec=pltpu.PrefetchScalarGridSpec(
            num_scalar_prefetch=1,
            grid=(n_dp,),
            in_specs=[pl.BlockSpec((width, model // n_dp), lambda j, place: (0, j)), whole, whole]
            + [
                pl.BlockSpec((rows // 4, tile), lambda j, place: (0, j))
                for tile in tiles
                for _ in range(6)
            ],
            out_specs=[whole, whole],
            scratch_shapes=[pltpu.VMEM((rows, width), F32)],
        ),
        out_shape=[jax.ShapeDtypeStruct((rows, width), BF16)] * 2,
        cost_estimate=pl.CostEstimate(
            flops=2 * rows * width * model,
            bytes_accessed=2 * width * model + 3 * rows * model + 8 * rows * width,
            transcendentals=rows * width,
        ),
        compiler_params=pltpu.CompilerParams(vmem_limit_bytes=VMEM_BYTES),
        name="input_grads",
    )(place, weight, gate_pre, up_pre, *(b for blocks in parts for b in blocks))


def add(*terms):
    return functools.reduce(lambda a, b: a + b, [t.astype(F32) for t in terms])


def line_body(n_dp, n_tensor, gate_pre, up_pre, down_weight, grad_out):
    place_z = lax.axis_index("tensor")
    me = lax.axis_index("dp")
    outer = jnp.bitwise_xor(place_z, 1)
    edge = (place_z == 0) | (place_z == 3)
    other_mid = jnp.where(edge, 3 - outer, 3 - place_z)
    other_edge = jnp.where(edge, 3 - place_z, 3 - outer)
    place = jnp.stack([place_z, outer, other_mid, other_edge, edge.astype(jnp.int32), me]).astype(jnp.int32)
    rows, model = gate_pre.shape[0], grad_out.shape[1]
    scale = 1.0 / math.sqrt(rows * n_dp)

    def along(pairs):
        return lambda v: lax.ppermute(v, "tensor", pairs)

    both, outward, inward, middle = along(OUTER), along(OUTWARD), along(INWARD), along(MIDDLE)

    def flip(bit):
        return lambda v: lax.ppermute(v, "dp", [(i, i ^ bit) for i in range(n_dp)])

    flip_core, flip_x, flip_y = flip(1), flip(2), flip(4)

    share = model // n_dp
    half = share // 2
    parts = []
    for c in range(2):
        own = jnp.concatenate(
            [grad_out[:, j * share + c * half : j * share + (c + 1) * half] for j in range(n_dp)], axis=1
        )
        parts.append([own, both(own), middle(own)])
    hidden, turned = hidden_of(place, gate_pre, up_pre)
    partial = forward_of(hidden, down_weight)
    for part in parts:
        own, p1, q1 = part
        p2 = outward(q1)
        q2 = middle(p1)
        p3 = outward(q2)
        part[:] = [own, p1, p2, q1, p3, q2]

    r1 = inward(partial[3])
    r2 = inward(partial[2])
    m1 = middle(add(partial[3], r1).astype(BF16))
    m2 = middle(add(partial[2], r2).astype(BF16))
    r3 = both(add(partial[1], m1).astype(BF16))
    ffn_out = add(partial[0], r3, m2).astype(BF16)

    columns = []
    for part in parts:
        send = weight_grad_of(place, turned, part, scale, 1, n_dp)
        got = flip_core(send)
        keep = weight_grad_of(place, turned, part, scale, 0, n_dp)
        top = keep.shape[1] // 2
        x_out = add(keep[1::2, :top], got[1::2, :top]).astype(BF16)
        y_out = add(keep[2:, top:], got[2:, top:]).astype(BF16)
        x_in = flip_x(x_out)
        y_in = flip_y(y_out)
        x_then_y = flip_y(add(keep[2, :top], got[2, :top], x_in[1]).astype(BF16))
        y_then_x = flip_x(add(keep[1, top:], got[1, top:], y_in[1]).astype(BF16))
        columns.append(
            jnp.concatenate(
                [
                    add(keep[0, :top], got[0, :top], x_in[0], x_then_y),
                    add(keep[0, top:], got[0, top:], y_in[0], y_then_x),
                ],
                axis=0,
            )
        )
    grad_down = jnp.concatenate(columns, axis=1)
    grad_gate, grad_up = input_grads_of(place, down_weight, gate_pre, up_pre, parts, n_dp)
    return (ffn_out, grad_gate, grad_up, grad_down)


def solution(mesh):
    n_dp, n_tensor = mesh.shape["dp"], mesh.shape["tensor"]
    on_line = n_dp == 8 and n_tensor == 4
    return jax.shard_map(
        functools.partial(line_body, n_dp, n_tensor) if on_line else plain_body,
        mesh=mesh,
        in_specs=(
            P("dp", "tensor"),
            P("dp", "tensor"),
            P("tensor", None),
            P(("dp", "tensor"), None),
        ),
        out_specs=(
            P(("dp", "tensor"), None),
            P("dp", "tensor"),
            P("dp", "tensor"),
            P("tensor", "dp"),
        ),
        check_vma=False,
    )
```

```python
import functools
import math

import jax
import jax.numpy as jnp
from jax import lax
from jax.experimental import pallas as pl
from jax.experimental.pallas import tpu as pltpu
from jax.sharding import PartitionSpec as P

F32, BF16 = jnp.float32, jnp.bfloat16

VMEM_BYTES = 28 * 1024 * 1024


def cost(us):
    return pl.CostEstimate(flops=int(1+us * 0.35e9), bytes_accessed=1, transcendentals=0)


def plain_body(gate_pre, up_pre, down_weight, grad_out):
    gate_val = gate_pre.astype(F32)
    up_val = up_pre.astype(F32)
    sigmoid_gate = jax.nn.sigmoid(gate_val)
    activated = gate_val * sigmoid_gate
    hidden = (activated * up_val).astype(BF16)
    grad_scale = 1.0 / math.sqrt(hidden.shape[0] * lax.axis_size("dp"))
    ffn_out = lax.psum_scatter(
        jnp.dot(hidden, down_weight, preferred_element_type=F32).astype(BF16),
        "tensor",
        scatter_dimension=0,
        tiled=True,
    )
    piece = lax.all_gather(grad_out, "tensor", axis=0, tiled=True)
    hidden_grad = jnp.einsum("td,fd->tf", piece, down_weight, preferred_element_type=F32)
    weight_grad = jnp.einsum("tf,td->fd", hidden, piece, preferred_element_type=F32)
    grad_down = lax.psum_scatter(
        (weight_grad * grad_scale).astype(BF16), "dp", scatter_dimension=1, tiled=True
    ).astype(F32)
    grad_gate = (
        hidden_grad * up_val * sigmoid_gate * (1.0 + gate_val * (1.0 - sigmoid_gate))
    ).astype(BF16)
    grad_up = (hidden_grad * activated).astype(BF16)
    return (ffn_out, grad_gate, grad_up, grad_down)


OUTER = [(0, 1), (1, 0), (2, 3), (3, 2)]
OUTWARD = [(1, 0), (2, 3)]
INWARD = [(0, 1), (3, 2)]
MIDDLE = [(1, 2), (2, 1)]


def forward_kernel(place, gate_ref, up_ref, weight_ref, turned_ref, *refs):
    out_refs, hidden_ref = refs[:4], refs[4]
    block = out_refs[0].shape[0]

    @pl.when(pl.program_id(0) == 0)
    def _():
        for i in range(4):
            rows = pl.ds(pl.multiple_of(place[i] * block, block), block)
            gate_val = gate_ref[rows].astype(F32)
            hidden = gate_val * jax.nn.sigmoid(gate_val) * up_ref[rows].astype(F32)
            hidden_ref[i * block : (i + 1) * block] = hidden.astype(BF16)
            turned_ref[:, i * block : (i + 1) * block] = hidden.T.astype(BF16)

    product = jnp.dot(hidden_ref[...], weight_ref[...], preferred_element_type=F32)
    for i, out_ref in enumerate(out_refs):
        out_ref[...] = product[i * block : (i + 1) * block].astype(BF16)


def forward_of(place, gate_pre, up_pre, weight, tile=1024):
    rows, width = gate_pre.shape
    model = weight.shape[1]
    block = rows // 4
    whole = pl.BlockSpec((rows, width), lambda j, place: (0, 0))
    return pl.pallas_call(
        forward_kernel,
        grid_spec=pltpu.PrefetchScalarGridSpec(
            num_scalar_prefetch=1,
            grid=(model // tile,),
            in_specs=[whole, whole, pl.BlockSpec((width, tile), lambda j, place: (0, j))],
            out_specs=[pl.BlockSpec((width, rows), lambda j, place: (0, 0))]
            + [pl.BlockSpec((block, tile), lambda j, place: (0, j))] * 4,
            scratch_shapes=[pltpu.VMEM((rows, width), BF16)],
        ),
        out_shape=[jax.ShapeDtypeStruct((width, rows), BF16)] + [jax.ShapeDtypeStruct((block, model), BF16)] * 4,
        cost_estimate=cost(9),
        compiler_params=pltpu.CompilerParams(vmem_limit_bytes=VMEM_BYTES),
        name="forward",
    )(place, gate_pre, up_pre, weight)


def split_kernel(tiles, in_ref, *out_refs):
    share = sum(tiles)
    for j in range(in_ref.shape[1] // share):
        start = j * share
        for out_ref, tile in zip(out_refs, tiles):
            out_ref[:, j * tile : (j + 1) * tile] = in_ref[:, start : start + tile]
            start += tile


def split(block, tiles):
    rows, columns = block.shape
    return pl.pallas_call(
        functools.partial(split_kernel, tiles),
        out_shape=[jax.ShapeDtypeStruct((rows, columns * t // sum(tiles)), BF16) for t in tiles],
        cost_estimate=cost(1),
        compiler_params=pltpu.CompilerParams(vmem_limit_bytes=VMEM_BYTES),
        name="split",
    )(block)


def weight_kernel(scale, place, turned_ref, own, outer, mid_e, mid_m, far_e, far_m, *out_refs):
    edge = place[4] == 1
    piece = jnp.concatenate(
        [own[...], outer[...], jnp.where(edge, mid_e[...], mid_m[...]), jnp.where(edge, far_e[...], far_m[...])],
        axis=0,
    )
    product = (jnp.dot(turned_ref[...], piece, preferred_element_type=F32) * scale).astype(BF16)
    for i, out_ref in enumerate(out_refs):

        @pl.when(pl.program_id(0) == i)
        def _():
            out_ref[...] = product


def weight_grad_of(place, turned, whole, far, c, scale, odd, n_dp):
    width, rows = turned.shape
    block, columns = far[0].shape
    tile = columns // n_dp
    n_parts = whole[0].shape[1] // columns

    def device(i, place):
        return jnp.bitwise_xor(place[5], 2 * i + odd)

    return pl.pallas_call(
        functools.partial(weight_kernel, scale),
        grid_spec=pltpu.PrefetchScalarGridSpec(
            num_scalar_prefetch=1,
            grid=(n_dp // 2,),
            in_specs=[pl.BlockSpec((width, rows), lambda i, place: (0, 0))]
            + [pl.BlockSpec((block, tile), lambda i, place: (0, n_parts * device(i, place) + c))] * 4
            + [pl.BlockSpec((block, tile), lambda i, place: (0, device(i, place)))] * 2,
            out_specs=[pl.BlockSpec((width, tile), lambda i, place: (0, 0))] * (n_dp // 2),
        ),
        out_shape=[jax.ShapeDtypeStruct((width, tile), BF16)] * (n_dp // 2),
        cost_estimate=cost(4),
        compiler_params=pltpu.CompilerParams(vmem_limit_bytes=VMEM_BYTES),
        name="weight_grad",
    )(place, turned, *whole, *far)


def input_kernel(n_dp, base, place, weight_ref, gate_ref, up_ref, *refs):
    step = pl.program_id(0)
    grad_gate_ref, grad_up_ref, total_ref = refs[-3:]
    edge = place[4] == 1
    if base == 0:
        pieces = [refs[0][...], refs[1][...]]
    else:
        far = [jnp.where(edge, refs[i][...], refs[i + 1][...]) for i in (2, 4)]
        pieces = [jnp.where(edge, refs[0][...], refs[1][...]), jnp.concatenate(far, axis=1)]
    part = lax.dot_general(
        weight_ref[...], jnp.concatenate(pieces, axis=0), (((1,), (1,)), ((), ())), preferred_element_type=F32
    )

    @pl.when(step == 0)
    def _():
        total_ref[...] = part

    @pl.when(step > 0)
    def _():
        total_ref[...] += part

    @pl.when(step == n_dp - 1)
    def _():
        block = refs[0].shape[0]
        for i in range(2):
            rows = pl.ds(pl.multiple_of(place[base + i] * block, block), block)
            hidden_grad = total_ref[:, i * block : (i + 1) * block].T
            gate_val = gate_ref[rows].astype(F32)
            up_val = up_ref[rows].astype(F32)
            s = jax.nn.sigmoid(gate_val)
            grad_gate_ref[rows] = (hidden_grad * up_val * s * (1.0 + gate_val * (1.0 - s))).astype(BF16)
            grad_up_ref[rows] = (hidden_grad * (gate_val * s)).astype(BF16)
            if base > 0:
                rows = pl.ds(pl.multiple_of(place[i] * block, block), block)
                grad_gate_ref[rows] = refs[6][rows]
                grad_up_ref[rows] = refs[7][rows]


def input_grads_of(place, weight, gate_pre, up_pre, blocks, n_dp, earlier=()):
    rows, width = gate_pre.shape
    model = weight.shape[1]
    base = 2 if earlier else 0
    whole = pl.BlockSpec((rows, width), lambda j, place: (0, 0))
    return pl.pallas_call(
        functools.partial(input_kernel, n_dp, base),
        grid_spec=pltpu.PrefetchScalarGridSpec(
            num_scalar_prefetch=1,
            grid=(n_dp,),
            in_specs=[pl.BlockSpec((width, model // n_dp), lambda j, place: (0, j)), whole, whole]
            + [pl.BlockSpec((rows // 4, b.shape[1] // n_dp), lambda j, place: (0, j)) for b in blocks]
            + [whole] * len(earlier),
            out_specs=[whole, whole],
            scratch_shapes=[pltpu.VMEM((width, rows // 2), F32)],
        ),
        out_shape=[jax.ShapeDtypeStruct((rows, width), BF16)] * 2,
        cost_estimate=cost(9),
        compiler_params=pltpu.CompilerParams(vmem_limit_bytes=VMEM_BYTES),
        name="input_grads",
    )(place, weight, gate_pre, up_pre, *blocks, *earlier)


def add(*terms):
    return functools.reduce(lambda a, b: a + b, [t.astype(F32) for t in terms])


def line_body(n_dp, n_tensor, gate_pre, up_pre, down_weight, grad_out):
    place_z = lax.axis_index("tensor")
    me = lax.axis_index("dp")
    outer = jnp.bitwise_xor(place_z, 1)
    edge = (place_z == 0) | (place_z == 3)
    other_mid = jnp.where(edge, 3 - outer, 3 - place_z)
    other_edge = jnp.where(edge, 3 - place_z, 3 - outer)
    place = jnp.stack([place_z, outer, other_mid, other_edge, edge.astype(jnp.int32), me]).astype(jnp.int32)
    rows, model = gate_pre.shape[0], grad_out.shape[1]
    scale = 1.0 / math.sqrt(rows * n_dp)

    def along(pairs):
        return lambda v: lax.ppermute(v, "tensor", pairs)

    both, outward, inward, middle = along(OUTER), along(OUTWARD), along(INWARD), along(MIDDLE)

    def flip(bit):
        return lambda v: lax.ppermute(v, "dp", [(i, i ^ bit) for i in range(n_dp)])

    flip_core, flip_x, flip_y = flip(1), flip(2), flip(4)

    def after(value, *done):
        return lax.optimization_barrier((value, *done))[0]

    def after(value, *done):
        return lax.optimization_barrier((value, *done))[0]

    share = model // n_dp
    half = share // 2
    p1, q1 = both(grad_out), middle(grad_out)
    turned, *partial = forward_of(place, gate_pre, up_pre, down_weight)
    p2 = outward(after(q1, partial[0]))
    p1a, p1b = split(p1, (half, half))
    q2a, q2b = middle(p1a), middle(p1b)
    r1 = inward(partial[3])
    s1 = add(partial[3], r1).astype(BF16)
    m1 = middle(s1)
    r2 = inward(after(partial[2], s1))
    early = input_grads_of(place, after(down_weight, q2a, s1), gate_pre, up_pre, [grad_out, p1], n_dp)
    p3a = outward(after(q2a, s1))
    p3b = outward(q2b)
    whole = [grad_out, p1, p2, q1]

    def weight_grad(c, far, *done):
        return weight_grad_of(place, after(turned, *done), whole, far, c, scale, 1, n_dp)

    def keep_of(c, far, *done):
        return weight_grad_of(place, after(turned, *done), whole, far, c, scale, 0, n_dp)

    top = gate_pre.shape[1] // 2

    def first(got, keep):
        x_out = jnp.stack([add(keep[i][:top], got[i][:top]).astype(BF16) for i in (1, 3)])
        y_out = jnp.stack([add(keep[i][top:], got[i][top:]).astype(BF16) for i in (2, 3)])
        return x_out, y_out

    def second(got, keep, x_in, y_in):
        x_then_y = add(keep[2][:top], got[2][:top], x_in[1]).astype(BF16)
        y_then_x = add(keep[1][top:], got[1][top:], y_in[1]).astype(BF16)
        return x_then_y, y_then_x

    def last(got, keep, x_in, y_in, x_then_y, y_then_x):
        return jnp.concatenate(
            [
                add(keep[0][:top], got[0][:top], x_in[0], x_then_y),
                add(keep[0][top:], got[0][top:], y_in[0], y_then_x),
            ],
            axis=0,
        )

    far_a, far_b = [p3a, after(q2a, q2b)], [p3b, q2b]
    send_a = weight_grad(0, far_a, early[0])
    got_a = [flip_core(v) for v in send_a]
    keep_a = keep_of(0, far_a, send_a[0])
    out_a = first(got_a, keep_a)
    in_a = flip_x(out_a[0]), flip_y(out_a[1])
    s2 = add(partial[2], after(r2, *out_a)).astype(BF16)
    m2 = middle(s2)
    send_b = weight_grad(1, [after(p3b, *out_a), q2b])
    got_b = [flip_core(v) for v in send_b]
    s3 = add(partial[1], after(m1, p3b)).astype(BF16)
    r3 = both(s3)
    on_a = second(got_a, keep_a, *after(in_a, send_b[0]))
    last_a = flip_y(on_a[0]), flip_x(on_a[1])
    keep_b = keep_of(1, far_b, *on_a)
    out_b = first(got_b, after(keep_b, s2, s3))
    in_b = flip_x(out_b[0]), flip_y(out_b[1])
    grad_gate, grad_up = input_grads_of(
        place, after(down_weight, *out_b), gate_pre, up_pre, [p2, q1, p3a, q2a, p3b, q2b], n_dp, earlier=early
    )
    on_b = second(got_b, keep_b, *after(in_b, grad_up))
    last_b = flip_y(on_b[0]), flip_x(on_b[1])
    ffn_out = add(partial[0], after(r3, *on_b), m2).astype(BF16)
    grad_down = jnp.concatenate(
        [last(got_a, keep_a, *in_a, *after(last_a, ffn_out)), last(got_b, keep_b, *in_b, *last_b)], axis=1
    )
    return (ffn_out, grad_gate, grad_up, grad_down)


def solution(mesh):
    n_dp, n_tensor = mesh.shape["dp"], mesh.shape["tensor"]
    on_line = n_dp == 8 and n_tensor == 4
    return jax.shard_map(
        functools.partial(line_body, n_dp, n_tensor) if on_line else plain_body,
        mesh=mesh,
        in_specs=(
            P("dp", "tensor"),
            P("dp", "tensor"),
            P("tensor", None),
            P(("dp", "tensor"), None),
        ),
        out_specs=(
            P(("dp", "tensor"), None),
            P("dp", "tensor"),
            P("dp", "tensor"),
            P("tensor", "dp"),
        ),
        check_vma=False,
    )
```

```python
import functools
import math

import jax
import jax.numpy as jnp
from jax import lax
from jax.experimental import pallas as pl
from jax.experimental.pallas import tpu as pltpu
from jax.sharding import PartitionSpec as P

F32, BF16 = jnp.float32, jnp.bfloat16

VMEM_BYTES = 28 * 1024 * 1024


def cost(us):
    return pl.CostEstimate(flops=int(us * 0.35e9), bytes_accessed=1, transcendentals=0)


def plain_body(gate_pre, up_pre, down_weight, grad_out):
    gate_val = gate_pre.astype(F32)
    up_val = up_pre.astype(F32)
    sigmoid_gate = jax.nn.sigmoid(gate_val)
    activated = gate_val * sigmoid_gate
    hidden = (activated * up_val).astype(BF16)
    grad_scale = 1.0 / math.sqrt(hidden.shape[0] * lax.axis_size("dp"))
    ffn_out = lax.psum_scatter(
        jnp.dot(hidden, down_weight, preferred_element_type=F32).astype(BF16),
        "tensor",
        scatter_dimension=0,
        tiled=True,
    )
    piece = lax.all_gather(grad_out, "tensor", axis=0, tiled=True)
    hidden_grad = jnp.einsum("td,fd->tf", piece, down_weight, preferred_element_type=F32)
    weight_grad = jnp.einsum("tf,td->fd", hidden, piece, preferred_element_type=F32)
    grad_down = lax.psum_scatter(
        (weight_grad * grad_scale).astype(BF16), "dp", scatter_dimension=1, tiled=True
    ).astype(F32)
    grad_gate = (
        hidden_grad * up_val * sigmoid_gate * (1.0 + gate_val * (1.0 - sigmoid_gate))
    ).astype(BF16)
    grad_up = (hidden_grad * activated).astype(BF16)
    return (ffn_out, grad_gate, grad_up, grad_down)


OUTER = [(0, 1), (1, 0), (2, 3), (3, 2)]
OUTWARD = [(1, 0), (2, 3)]
INWARD = [(0, 1), (3, 2)]
MIDDLE = [(1, 2), (2, 1)]


def forward_kernel(place, gate_ref, up_ref, weight_ref, turned_ref, *refs):
    out_refs, hidden_ref = refs[:4], refs[4]
    block = out_refs[0].shape[0]

    @pl.when(pl.program_id(0) == 0)
    def _():
        for i in range(4):
            rows = pl.ds(pl.multiple_of(place[i] * block, block), block)
            gate_val = gate_ref[rows].astype(F32)
            hidden = gate_val * jax.nn.sigmoid(gate_val) * up_ref[rows].astype(F32)
            hidden_ref[i * block : (i + 1) * block] = hidden.astype(BF16)
            turned_ref[:, i * block : (i + 1) * block] = hidden.T.astype(BF16)

    product = jnp.dot(hidden_ref[...], weight_ref[...], preferred_element_type=F32)
    for i, out_ref in enumerate(out_refs):
        out_ref[...] = product[i * block : (i + 1) * block].astype(BF16)


def forward_of(place, gate_pre, up_pre, weight, tile=1024):
    rows, width = gate_pre.shape
    model = weight.shape[1]
    block = rows // 4
    whole = pl.BlockSpec((rows, width), lambda j, place: (0, 0))
    return pl.pallas_call(
        forward_kernel,
        grid_spec=pltpu.PrefetchScalarGridSpec(
            num_scalar_prefetch=1,
            grid=(model // tile,),
            in_specs=[whole, whole, pl.BlockSpec((width, tile), lambda j, place: (0, j))],
            out_specs=[pl.BlockSpec((width, rows), lambda j, place: (0, 0))]
            + [pl.BlockSpec((block, tile), lambda j, place: (0, j))] * 4,
            scratch_shapes=[pltpu.VMEM((rows, width), BF16)],
        ),
        out_shape=[jax.ShapeDtypeStruct((width, rows), BF16)] + [jax.ShapeDtypeStruct((block, model), BF16)] * 4,
        cost_estimate=cost(9),
        compiler_params=pltpu.CompilerParams(vmem_limit_bytes=VMEM_BYTES),
        name="forward",
    )(place, gate_pre, up_pre, weight)


def split_kernel(tiles, in_ref, *out_refs):
    share = sum(tiles)
    for j in range(in_ref.shape[1] // share):
        start = j * share
        for out_ref, tile in zip(out_refs, tiles):
            out_ref[:, j * tile : (j + 1) * tile] = in_ref[:, start : start + tile]
            start += tile


def split(block, tiles):
    rows, columns = block.shape
    return pl.pallas_call(
        functools.partial(split_kernel, tiles),
        out_shape=[jax.ShapeDtypeStruct((rows, columns * t // sum(tiles)), BF16) for t in tiles],
        cost_estimate=cost(1),
        compiler_params=pltpu.CompilerParams(vmem_limit_bytes=VMEM_BYTES),
        name="split",
    )(block)


def weight_kernel(scale, place, turned_ref, own, outer, mid_e, mid_m, far_e, far_m, *out_refs):
    edge = place[4] == 1
    piece = jnp.concatenate(
        [own[...], outer[...], jnp.where(edge, mid_e[...], mid_m[...]), jnp.where(edge, far_e[...], far_m[...])],
        axis=0,
    )
    product = (jnp.dot(turned_ref[...], piece, preferred_element_type=F32) * scale).astype(BF16)
    for i, out_ref in enumerate(out_refs):

        @pl.when(pl.program_id(0) == i)
        def _():
            out_ref[...] = product


def weight_grad_of(place, turned, whole, far, c, scale, cores, n_dp):
    width, rows = turned.shape
    block, columns = far[0].shape
    tile = columns // n_dp
    n_parts = whole[0].shape[1] // columns
    n_out = n_dp // 2

    def device(j, place):
        core = cores[0] if len(cores) == 1 else jnp.where(j < n_out, cores[0], cores[1])
        return jnp.bitwise_xor(place[5], 2 * lax.rem(j, n_out) + core)

    outs = pl.pallas_call(
        functools.partial(weight_kernel, scale),
        grid_spec=pltpu.PrefetchScalarGridSpec(
            num_scalar_prefetch=1,
            grid=(n_out * len(cores),),
            in_specs=[pl.BlockSpec((width, rows), lambda j, place: (0, 0))]
            + [pl.BlockSpec((block, tile), lambda j, place: (0, n_parts * device(j, place) + c))] * 4
            + [pl.BlockSpec((block, tile), lambda j, place: (0, device(j, place)))] * 2,
            out_specs=[pl.BlockSpec((width, tile), lambda j, place: (0, 0))] * (n_out * len(cores)),
        ),
        out_shape=[jax.ShapeDtypeStruct((width, tile), BF16)] * (n_out * len(cores)),
        cost_estimate=cost(4),
        compiler_params=pltpu.CompilerParams(vmem_limit_bytes=VMEM_BYTES),
        name="weight_grad",
    )(place, turned, *whole, *far)
    return [outs[k * n_out : (k + 1) * n_out] for k in range(len(cores))]


def input_kernel(n_dp, base, place, weight_ref, gate_ref, up_ref, *refs):
    step = pl.program_id(0)
    grad_gate_ref, grad_up_ref, total_ref = refs[-3:]
    edge = place[4] == 1
    if base == 0:
        pieces = [refs[0][...], refs[1][...]]
    else:
        far = [jnp.where(edge, refs[i][...], refs[i + 1][...]) for i in (2, 4)]
        pieces = [jnp.where(edge, refs[0][...], refs[1][...]), jnp.concatenate(far, axis=1)]
    part = lax.dot_general(
        weight_ref[...], jnp.concatenate(pieces, axis=0), (((1,), (1,)), ((), ())), preferred_element_type=F32
    )

    @pl.when(step == 0)
    def _():
        total_ref[...] = part

    @pl.when(step > 0)
    def _():
        total_ref[...] += part

    @pl.when(step == n_dp - 1)
    def _():
        block = refs[0].shape[0]
        for i in range(2):
            rows = pl.ds(pl.multiple_of(place[base + i] * block, block), block)
            hidden_grad = total_ref[:, i * block : (i + 1) * block].T
            gate_val = gate_ref[rows].astype(F32)
            up_val = up_ref[rows].astype(F32)
            s = jax.nn.sigmoid(gate_val)
            grad_gate_ref[rows] = (hidden_grad * up_val * s * (1.0 + gate_val * (1.0 - s))).astype(BF16)
            grad_up_ref[rows] = (hidden_grad * (gate_val * s)).astype(BF16)
            if base > 0:
                rows = pl.ds(pl.multiple_of(place[i] * block, block), block)
                grad_gate_ref[rows] = refs[6][rows]
                grad_up_ref[rows] = refs[7][rows]


def input_grads_of(place, weight, gate_pre, up_pre, blocks, n_dp, earlier=()):
    rows, width = gate_pre.shape
    model = weight.shape[1]
    base = 2 if earlier else 0
    whole = pl.BlockSpec((rows, width), lambda j, place: (0, 0))
    return pl.pallas_call(
        functools.partial(input_kernel, n_dp, base),
        grid_spec=pltpu.PrefetchScalarGridSpec(
            num_scalar_prefetch=1,
            grid=(n_dp,),
            in_specs=[pl.BlockSpec((width, model // n_dp), lambda j, place: (0, j)), whole, whole]
            + [pl.BlockSpec((rows // 4, b.shape[1] // n_dp), lambda j, place: (0, j)) for b in blocks]
            + [whole] * len(earlier),
            out_specs=[whole, whole],
            scratch_shapes=[pltpu.VMEM((width, rows // 2), F32)],
        ),
        out_shape=[jax.ShapeDtypeStruct((rows, width), BF16)] * 2,
        cost_estimate=cost(9),
        compiler_params=pltpu.CompilerParams(vmem_limit_bytes=VMEM_BYTES),
        name="input_grads",
    )(place, weight, gate_pre, up_pre, *blocks, *earlier)


def add(*terms):
    return functools.reduce(lambda a, b: a + b, [t.astype(F32) for t in terms])


def line_body(n_dp, n_tensor, gate_pre, up_pre, down_weight, grad_out):
    place_z = lax.axis_index("tensor")
    me = lax.axis_index("dp")
    outer = jnp.bitwise_xor(place_z, 1)
    edge = (place_z == 0) | (place_z == 3)
    other_mid = jnp.where(edge, 3 - outer, 3 - place_z)
    other_edge = jnp.where(edge, 3 - place_z, 3 - outer)
    place = jnp.stack([place_z, outer, other_mid, other_edge, edge.astype(jnp.int32), me]).astype(jnp.int32)
    rows, model = gate_pre.shape[0], grad_out.shape[1]
    scale = 1.0 / math.sqrt(rows * n_dp)

    def along(pairs):
        return lambda v: lax.ppermute(v, "tensor", pairs)

    both, outward, inward, middle = along(OUTER), along(OUTWARD), along(INWARD), along(MIDDLE)

    def flip(bit):
        return lambda v: lax.ppermute(v, "dp", [(i, i ^ bit) for i in range(n_dp)])

    flip_core, flip_x, flip_y = flip(1), flip(2), flip(4)

    def after(value, *done):
        return lax.optimization_barrier((value, *done))[0]

    share = model // n_dp
    half = share // 2
    p1, q1 = both(grad_out), middle(grad_out)
    turned, *partial = forward_of(place, gate_pre, up_pre, down_weight)
    p2 = outward(after(q1, partial[0]))
    q2 = middle(after(p1, partial[0]))
    r1 = inward(partial[3])
    s1 = add(partial[3], r1).astype(BF16)
    q2a, q2b = split(q2, (half, half))
    m1 = middle(s1)
    r2 = inward(after(partial[2], s1))
    early = input_grads_of(place, after(down_weight, q2a, s1), gate_pre, up_pre, [grad_out, p1], n_dp)
    p3a = outward(after(q2a, s1))
    p3b = outward(q2b)
    whole = [grad_out, p1, p2, q1]

    top = gate_pre.shape[1] // 2

    def first(got, keep):
        x_out = jnp.stack([add(keep[i][:top], got[i][:top]).astype(BF16) for i in (1, 3)])
        y_out = jnp.stack([add(keep[i][top:], got[i][top:]).astype(BF16) for i in (2, 3)])
        return x_out, y_out

    def second(got, keep, x_in, y_in):
        x_then_y = add(keep[2][:top], got[2][:top], x_in[1]).astype(BF16)
        y_then_x = add(keep[1][top:], got[1][top:], y_in[1]).astype(BF16)
        return x_then_y, y_then_x

    def last(got, keep, x_in, y_in, x_then_y, y_then_x):
        return jnp.concatenate(
            [
                add(keep[0][:top], got[0][:top], x_in[0], x_then_y),
                add(keep[0][top:], got[0][top:], y_in[0], y_then_x),
            ],
            axis=0,
        )

    def flip_cores(send):
        pairs = [flip_core(jnp.stack(send[i : i + 2])) for i in range(0, len(send), 2)]
        return [pair[k] for pair in pairs for k in range(2)]

    far_a, far_b = [p3a, after(q2a, q2b)], [p3b, q2b]
    send_a, keep_a = weight_grad_of(place, after(turned, early[0]), whole, far_a, 0, scale, (1, 0), n_dp)
    got_a = flip_cores(send_a)
    out_a = first(got_a, keep_a)
    in_a = flip_x(out_a[0]), flip_y(out_a[1])
    (send_b,) = weight_grad_of(place, turned, whole, [after(p3b, *out_a), q2b], 1, scale, (1,), n_dp)
    got_b = flip_cores(send_b)
    s2 = add(partial[2], after(r2, send_b[0])).astype(BF16)
    m2 = middle(s2)
    s3 = add(partial[1], after(m1, p3b)).astype(BF16)
    r3 = both(s3)
    (keep_b,) = weight_grad_of(place, after(turned, send_b[0]), whole, far_b, 1, scale, (0,), n_dp)
    out_b = first(got_b, after(keep_b, s2, s3))
    in_b = flip_x(out_b[0]), flip_y(out_b[1])
    on_a = second(got_a, keep_a, *after(in_a, *out_b))
    last_a = flip_y(on_a[0]), flip_x(on_a[1])
    grad_gate, grad_up = input_grads_of(
        place, after(down_weight, *out_b), gate_pre, up_pre, [p2, q1, p3a, q2a, p3b, q2b], n_dp, earlier=early
    )
    on_b = second(got_b, keep_b, *after(in_b, grad_up))
    last_b = flip_y(on_b[0]), flip_x(on_b[1])
    ffn_out = add(partial[0], after(r3, *on_b), m2).astype(BF16)
    grad_down = jnp.concatenate(
        [last(got_a, keep_a, *in_a, *after(last_a, ffn_out)), last(got_b, keep_b, *in_b, *last_b)], axis=1
    )
    return (ffn_out, grad_gate, grad_up, grad_down)


def solution(mesh):
    n_dp, n_tensor = mesh.shape["dp"], mesh.shape["tensor"]
    on_line = n_dp == 8 and n_tensor == 4
    return jax.shard_map(
        functools.partial(line_body, n_dp, n_tensor) if on_line else plain_body,
        mesh=mesh,
        in_specs=(
            P("dp", "tensor"),
            P("dp", "tensor"),
            P("tensor", None),
            P(("dp", "tensor"), None),
        ),
        out_specs=(
            P(("dp", "tensor"), None),
            P("dp", "tensor"),
            P("dp", "tensor"),
            P("tensor", "dp"),
        ),
        check_vma=False,
    )
```

```python
import functools
import math

import jax
import jax.numpy as jnp
from jax import lax
from jax.experimental import pallas as pl
from jax.experimental.pallas import tpu as pltpu
from jax.sharding import PartitionSpec as P

F32, BF16 = jnp.float32, jnp.bfloat16

VMEM_BYTES = 28 * 1024 * 1024


def cost(us):
    return pl.CostEstimate(flops=int(us * 0.35e9), bytes_accessed=1, transcendentals=0)


def plain_body(gate_pre, up_pre, down_weight, grad_out):
    gate_val = gate_pre.astype(F32)
    up_val = up_pre.astype(F32)
    sigmoid_gate = jax.nn.sigmoid(gate_val)
    activated = gate_val * sigmoid_gate
    hidden = (activated * up_val).astype(BF16)
    grad_scale = 1.0 / math.sqrt(hidden.shape[0] * lax.axis_size("dp"))
    ffn_out = lax.psum_scatter(
        jnp.dot(hidden, down_weight, preferred_element_type=F32).astype(BF16),
        "tensor",
        scatter_dimension=0,
        tiled=True,
    )
    piece = lax.all_gather(grad_out, "tensor", axis=0, tiled=True)
    hidden_grad = jnp.einsum("td,fd->tf", piece, down_weight, preferred_element_type=F32)
    weight_grad = jnp.einsum("tf,td->fd", hidden, piece, preferred_element_type=F32)
    grad_down = lax.psum_scatter(
        (weight_grad * grad_scale).astype(BF16), "dp", scatter_dimension=1, tiled=True
    ).astype(F32)
    grad_gate = (
        hidden_grad * up_val * sigmoid_gate * (1.0 + gate_val * (1.0 - sigmoid_gate))
    ).astype(BF16)
    grad_up = (hidden_grad * activated).astype(BF16)
    return (ffn_out, grad_gate, grad_up, grad_down)


OUTER = [(0, 1), (1, 0), (2, 3), (3, 2)]
OUTWARD = [(1, 0), (2, 3)]
INWARD = [(0, 1), (3, 2)]
MIDDLE = [(1, 2), (2, 1)]


def forward_kernel(place, gate_ref, up_ref, weight_ref, turned_ref, *refs):
    out_refs, hidden_ref = refs[:4], refs[4]
    block = out_refs[0].shape[0]

    @pl.when(pl.program_id(0) == 0)
    def _():
        for i in range(4):
            rows = pl.ds(pl.multiple_of(place[i] * block, block), block)
            gate_val = gate_ref[rows].astype(F32)
            hidden = gate_val * jax.nn.sigmoid(gate_val) * up_ref[rows].astype(F32)
            hidden_ref[i * block : (i + 1) * block] = hidden.astype(BF16)
            turned_ref[:, i * block : (i + 1) * block] = hidden.T.astype(BF16)

    product = jnp.dot(hidden_ref[...], weight_ref[...], preferred_element_type=F32)
    for i, out_ref in enumerate(out_refs):
        out_ref[...] = product[i * block : (i + 1) * block].astype(BF16)


def forward_of(place, gate_pre, up_pre, weight, tile=1024):
    rows, width = gate_pre.shape
    model = weight.shape[1]
    block = rows // 4
    whole = pl.BlockSpec((rows, width), lambda j, place: (0, 0))
    return pl.pallas_call(
        forward_kernel,
        grid_spec=pltpu.PrefetchScalarGridSpec(
            num_scalar_prefetch=1,
            grid=(model // tile,),
            in_specs=[whole, whole, pl.BlockSpec((width, tile), lambda j, place: (0, j))],
            out_specs=[pl.BlockSpec((width, rows), lambda j, place: (0, 0))]
            + [pl.BlockSpec((block, tile), lambda j, place: (0, j))] * 4,
            scratch_shapes=[pltpu.VMEM((rows, width), BF16)],
        ),
        out_shape=[jax.ShapeDtypeStruct((width, rows), BF16)] + [jax.ShapeDtypeStruct((block, model), BF16)] * 4,
        cost_estimate=cost(9),
        compiler_params=pltpu.CompilerParams(vmem_limit_bytes=VMEM_BYTES),
        name="forward",
    )(place, gate_pre, up_pre, weight)


def split_kernel(tiles, in_ref, *out_refs):
    share = sum(tiles)
    for j in range(in_ref.shape[1] // share):
        start = j * share
        for out_ref, tile in zip(out_refs, tiles):
            out_ref[:, j * tile : (j + 1) * tile] = in_ref[:, start : start + tile]
            start += tile


def split(block, tiles):
    rows, columns = block.shape
    return pl.pallas_call(
        functools.partial(split_kernel, tiles),
        out_shape=[jax.ShapeDtypeStruct((rows, columns * t // sum(tiles)), BF16) for t in tiles],
        cost_estimate=cost(1),
        compiler_params=pltpu.CompilerParams(vmem_limit_bytes=VMEM_BYTES),
        name="split",
    )(block)


def weight_kernel(scale, place, turned_ref, own, outer, mid_e, mid_m, far_e, far_m, *out_refs):
    edge = place[4] == 1
    piece = jnp.concatenate(
        [own[...], outer[...], jnp.where(edge, mid_e[...], mid_m[...]), jnp.where(edge, far_e[...], far_m[...])],
        axis=0,
    )
    product = (jnp.dot(turned_ref[...], piece, preferred_element_type=F32) * scale).astype(BF16)
    for i, out_ref in enumerate(out_refs):

        @pl.when(pl.program_id(0) == i)
        def _():
            out_ref[...] = product


def weight_grad_of(place, turned, whole, far, c, scale, cores, n_dp):
    width, rows = turned.shape
    block, columns = far[0].shape
    tile = columns // n_dp
    n_parts = whole[0].shape[1] // columns
    n_out = n_dp // 2

    def device(j, place):
        core = cores[0] if len(cores) == 1 else jnp.where(j < n_out, cores[0], cores[1])
        return jnp.bitwise_xor(place[5], 2 * lax.rem(j, n_out) + core)

    outs = pl.pallas_call(
        functools.partial(weight_kernel, scale),
        grid_spec=pltpu.PrefetchScalarGridSpec(
            num_scalar_prefetch=1,
            grid=(n_out * len(cores),),
            in_specs=[pl.BlockSpec((width, rows), lambda j, place: (0, 0))]
            + [pl.BlockSpec((block, tile), lambda j, place: (0, n_parts * device(j, place) + c))] * 4
            + [pl.BlockSpec((block, tile), lambda j, place: (0, device(j, place)))] * 2,
            out_specs=[pl.BlockSpec((width, tile), lambda j, place: (0, 0))] * (n_out * len(cores)),
        ),
        out_shape=[jax.ShapeDtypeStruct((width, tile), BF16)] * (n_out * len(cores)),
        cost_estimate=cost(4),
        compiler_params=pltpu.CompilerParams(vmem_limit_bytes=VMEM_BYTES),
        name="weight_grad",
    )(place, turned, *whole, *far)
    return [outs[k * n_out : (k + 1) * n_out] for k in range(len(cores))]


def input_kernel(n_dp, base, place, weight_ref, gate_ref, up_ref, *refs):
    step = pl.program_id(0)
    grad_gate_ref, grad_up_ref, total_ref = refs[-3:]
    edge = place[4] == 1
    if base == 0:
        pieces = [refs[0][...], refs[1][...]]
    else:
        far = [jnp.where(edge, refs[i][...], refs[i + 1][...]) for i in (2, 4)]
        pieces = [jnp.where(edge, refs[0][...], refs[1][...]), jnp.concatenate(far, axis=1)]
    part = lax.dot_general(
        weight_ref[...], jnp.concatenate(pieces, axis=0), (((1,), (1,)), ((), ())), preferred_element_type=F32
    )

    @pl.when(step == 0)
    def _():
        total_ref[...] = part

    @pl.when(step > 0)
    def _():
        total_ref[...] += part

    @pl.when(step == n_dp - 1)
    def _():
        block = refs[0].shape[0]
        for i in range(2):
            rows = pl.ds(pl.multiple_of(place[base + i] * block, block), block)
            hidden_grad = total_ref[:, i * block : (i + 1) * block].T
            gate_val = gate_ref[rows].astype(F32)
            up_val = up_ref[rows].astype(F32)
            s = jax.nn.sigmoid(gate_val)
            grad_gate_ref[rows] = (hidden_grad * up_val * s * (1.0 + gate_val * (1.0 - s))).astype(BF16)
            grad_up_ref[rows] = (hidden_grad * (gate_val * s)).astype(BF16)
            if base > 0:
                rows = pl.ds(pl.multiple_of(place[i] * block, block), block)
                grad_gate_ref[rows] = refs[6][rows]
                grad_up_ref[rows] = refs[7][rows]


def input_grads_of(place, weight, gate_pre, up_pre, blocks, n_dp, earlier=()):
    rows, width = gate_pre.shape
    model = weight.shape[1]
    base = 2 if earlier else 0
    whole = pl.BlockSpec((rows, width), lambda j, place: (0, 0))
    return pl.pallas_call(
        functools.partial(input_kernel, n_dp, base),
        grid_spec=pltpu.PrefetchScalarGridSpec(
            num_scalar_prefetch=1,
            grid=(n_dp,),
            in_specs=[pl.BlockSpec((width, model // n_dp), lambda j, place: (0, j)), whole, whole]
            + [pl.BlockSpec((rows // 4, b.shape[1] // n_dp), lambda j, place: (0, j)) for b in blocks]
            + [whole] * len(earlier),
            out_specs=[whole, whole],
            scratch_shapes=[pltpu.VMEM((width, rows // 2), F32)],
        ),
        out_shape=[jax.ShapeDtypeStruct((rows, width), BF16)] * 2,
        cost_estimate=cost(9),
        compiler_params=pltpu.CompilerParams(vmem_limit_bytes=VMEM_BYTES),
        name="input_grads",
    )(place, weight, gate_pre, up_pre, *blocks, *earlier)


def add(*terms):
    return functools.reduce(lambda a, b: a + b, [t.astype(F32) for t in terms])


def line_body(n_dp, n_tensor, gate_pre, up_pre, down_weight, grad_out):
    place_z = lax.axis_index("tensor")
    me = lax.axis_index("dp")
    outer = jnp.bitwise_xor(place_z, 1)
    edge = (place_z == 0) | (place_z == 3)
    other_mid = jnp.where(edge, 3 - outer, 3 - place_z)
    other_edge = jnp.where(edge, 3 - place_z, 3 - outer)
    place = jnp.stack([place_z, outer, other_mid, other_edge, edge.astype(jnp.int32), me]).astype(jnp.int32)
    rows, model = gate_pre.shape[0], grad_out.shape[1]
    scale = 1.0 / math.sqrt(rows * n_dp)

    def along(pairs):
        return lambda v: lax.ppermute(v, "tensor", pairs)

    both, outward, inward, middle = along(OUTER), along(OUTWARD), along(INWARD), along(MIDDLE)

    def flip(bit):
        return lambda v: lax.ppermute(v, "dp", [(i, i ^ bit) for i in range(n_dp)])

    flip_core, flip_x, flip_y = flip(1), flip(2), flip(4)

    def after(value, *done):
        return lax.optimization_barrier((value, *done))[0]

    share = model // n_dp
    half = share // 2
    p1, q1 = both(grad_out), middle(grad_out)
    turned, *partial = forward_of(place, gate_pre, up_pre, down_weight)
    p2 = outward(after(q1, partial[0]))
    q2 = middle(after(p1, partial[0]))
    r1 = inward(partial[3])
    s1 = add(partial[3], r1).astype(BF16)
    q2a, q2b = split(q2, (half, half))
    m1 = middle(s1)
    r2 = inward(after(partial[2], s1))
    early = input_grads_of(place, after(down_weight, q2a, s1), gate_pre, up_pre, [grad_out, p1], n_dp)
    p3a = outward(after(q2a, s1))
    p3b = outward(q2b)
    whole = [grad_out, p1, p2, q1]

    top = gate_pre.shape[1] // 2

    def first(got, keep):
        x_out = jnp.stack([add(keep[i][:top], got[i][:top]).astype(BF16) for i in (1, 3)])
        y_out = jnp.stack([add(keep[i][top:], got[i][top:]).astype(BF16) for i in (2, 3)])
        return x_out, y_out

    def second(got, keep, x_in, y_in):
        x_then_y = add(keep[2][:top], got[2][:top], x_in[1]).astype(BF16)
        y_then_x = add(keep[1][top:], got[1][top:], y_in[1]).astype(BF16)
        return x_then_y, y_then_x

    def last(got, keep, x_in, y_in, x_then_y, y_then_x):
        return jnp.concatenate(
            [
                add(keep[0][:top], got[0][:top], x_in[0], x_then_y),
                add(keep[0][top:], got[0][top:], y_in[0], y_then_x),
            ],
            axis=0,
        )

    def flip_cores(send):
        pairs = [flip_core(jnp.stack(send[i : i + 2])) for i in range(0, len(send), 2)]
        return [pair[k] for pair in pairs for k in range(2)]

    far_a, far_b = [p3a, after(q2a, q2b)], [p3b, q2b]
    send_a, keep_a = weight_grad_of(place, after(turned, early[0]), whole, far_a, 0, scale, (1, 0), n_dp)
    got_a = flip_cores(send_a)
    out_a = first(got_a, keep_a)
    in_a = flip_x(out_a[0]), flip_y(out_a[1])
    (send_b,) = weight_grad_of(place, turned, whole, [after(p3b, *out_a), q2b], 1, scale, (1,), n_dp)
    got_b = flip_cores(send_b)
    s2 = add(partial[2], after(r2, send_b[0])).astype(BF16)
    m2 = middle(s2)
    s3 = add(partial[1], m1).astype(BF16)
    r3 = both(s3)
    (keep_b,) = weight_grad_of(place, after(turned, send_b[0]), whole, far_b, 1, scale, (0,), n_dp)
    out_b = first(got_b, after(keep_b, s2, s3))
    in_b = flip_x(out_b[0]), flip_y(out_b[1])
    on_a = second(got_a, keep_a, *after(in_a, *out_b))
    last_a = flip_y(on_a[0]), flip_x(on_a[1])
    grad_gate, grad_up = input_grads_of(
        place, after(down_weight, *out_b), gate_pre, up_pre, [p2, q1, p3a, q2a, p3b, q2b], n_dp, earlier=early
    )
    on_b = second(got_b, keep_b, *after(in_b, grad_up))
    last_b = flip_y(on_b[0]), flip_x(on_b[1])
    ffn_out = add(partial[0], after(r3, *on_b), m2).astype(BF16)
    grad_down = jnp.concatenate(
        [last(got_a, keep_a, *in_a, *after(last_a, ffn_out)), last(got_b, keep_b, *in_b, *last_b)], axis=1
    )
    return (ffn_out, grad_gate, grad_up, grad_down)


def solution(mesh):
    n_dp, n_tensor = mesh.shape["dp"], mesh.shape["tensor"]
    on_line = n_dp == 8 and n_tensor == 4
    return jax.shard_map(
        functools.partial(line_body, n_dp, n_tensor) if on_line else plain_body,
        mesh=mesh,
        in_specs=(
            P("dp", "tensor"),
            P("dp", "tensor"),
            P("tensor", None),
            P(("dp", "tensor"), None),
        ),
        out_specs=(
            P(("dp", "tensor"), None),
            P("dp", "tensor"),
            P("dp", "tensor"),
            P("tensor", "dp"),
        ),
        check_vma=False,
    )
```
